32 devices in a mesh: groups: 2 (over y), expert: 4 (over x, core), mp: 4 (over z).
Axes of the slice: x: 2, y: 2, z: 4, core: 2. Of those that a mesh axis runs over, the one named last changes fastest.
Arguments:
- output_gradient: bfloat16 [2048, 6144], P(('groups', 'expert'), 'mp'), parts along dimension 0, may hold values from -1.5 to 1.5
- routes: int32 [2048, 2], P(('groups', 'expert')), parts along dimension 0, may hold values from 0 to 3, all different within a row; in each aligned block of 256 rows (0 to 255, 256 to 511, ...) at most 128 rows name the same one
- mixture_coefficients: bfloat16 [2048, 2], P(('groups', 'expert')), parts along dimension 0, may hold values from 0.099609375 to 0.8984375
- gate_preactivation: bfloat16 [4, 1024, 8192], P('expert', 'groups', 'mp'), parts along dimension 1, may hold values from -6 to 6
- up_projection_saved: bfloat16 [4, 1024, 8192], P('expert', 'groups', 'mp'), parts along dimension 1, may hold values from -6 to 6
- down_matrix: bfloat16 [4, 8192, 6144], P('expert', 'mp'), may hold values from -0.0625 to 0.0625
- lowrank_left_matrix: bfloat16 [4, 16, 8192], P('expert', None, 'mp'), may hold values from -0.0625 to 0.0625
- lowrank_right_matrix: bfloat16 [4, 16, 6144], P('expert'), may hold values from -0.078125 to 0.078125
Outputs:
- gate_grad: bfloat16 [4, 1024, 8192], P('expert', 'groups', 'mp'), parts along dimension 1
- up_grad: bfloat16 [4, 1024, 8192], P('expert', 'groups', 'mp'), parts along dimension 1
- lora_a_grad: float32 [8, 16, 8192], P(('groups', 'expert'), None, 'mp'), parts along dimension 0
- lora_b_grad: float32 [8, 16, 6144], P(('groups', 'expert'), None, 'mp'), parts along dimension 0
- weight_grad: float32 [2048, 2], P(('groups', 'expert')), parts along dimension 0
The draws below stay inside these ranges and needn't reach their ends.
There are 2 independent parts, one for each index of `groups`. The reference program is written for one: setup_inputs(seed, part) draws one part's arguments, and reference() takes and returns one part's arrays. A program takes and returns all parts, laid end to end along the dimension named above; an argument that names none is the same for every part. Nothing has to cross between parts.
Inputs may be any that keep to these rules, and one draw needn't show every extreme that they name: `routes`: each token names 2 different experts; the rows of one owner name no expert more than 128 times, a bound that some block reaches.
All inputs are finite; a program needn't handle non-finite values.
Results may differ from the reference program's by a relative error of at most 0.005.
Values may be sent and summed in bfloat16 or wider, within the bound.
A program may use at most 128 MiB of HBM per device.

```python
import math
import jax
import jax.numpy as jnp
import numpy as np
from jax import lax

EMBED_DIM = 6144
INNER_NEURONS = 8192
LOWRANK_DIM = 16
TOP = 2
TOK_DEV = 256
CAP = 128
SPECIALIST_TOTAL = 4
TOKENS = 1024
SLOTS = 512
N_EXPERT = 4


def block_levels(stream_key, dims, pieces, low, high):
    gain, own = 1.0, jax.random.fold_in(stream_key, 6)
    for axis_at, blocks in pieces:
        steps = jnp.exp(jax.random.uniform(jax.random.fold_in(own, axis_at), (blocks,), jnp.float32, low / len(pieces), high / len(pieces)))
        gain = gain * jnp.repeat(steps, dims[axis_at] // blocks).reshape([-1 if axis == axis_at else 1 for axis in range(len(dims))])
    return gain


def assign_block(rng, own, number, rows, count, top, most, skew):
    order = jax.random.permutation(rng, count)
    packed, usual = shares(count, rows * top, most, skew, True), shares(count, rows * top, most, skew, False)
    places = jnp.arange(count)

    def named(lengths, turn):
        used = int((lengths > 0).sum())
        fixed = max(1, used // 4)
        passed = fixed + (places - fixed + turn * (used - fixed)) % max(1, count - fixed)
        return jnp.zeros((count,), jnp.int32).at[order[jnp.where(places < fixed, places, passed)]].set(jnp.asarray(lengths, jnp.int32))

    lengths = jnp.where(number % 4 == 0, named(packed, number // 4), named(usual, number - number // 4 - 1))
    mixed = jax.random.permutation(jax.random.fold_in(own, 3), count)
    giver, receiver = mixed[0:count // 2 * 2:2], mixed[1:count // 2 * 2:2]
    margin = jnp.minimum(lengths[giver] - 1, most - lengths[receiver]) // 2
    margin = jnp.where((giver == order[0]) | (receiver == order[0]) | (lengths[receiver] == 0), 0, jnp.maximum(margin, 0))
    passed = jax.random.randint(jax.random.fold_in(own, 4), (count // 2,), 0, 1 << 20) % (margin + 1)
    lengths = lengths.at[giver].add(-passed).at[receiver].add(passed)
    members = jnp.searchsorted(jnp.cumsum(lengths), jnp.arange(rows * top), side="right").astype(jnp.int32)
    table = members.reshape(top, rows).T
    table = table[jax.random.permutation(jax.random.fold_in(own, 1), rows)]
    turn = jax.random.randint(jax.random.fold_in(own, 2), (rows, 1), 0, top)
    return jnp.take_along_axis(table, (jnp.arange(top)[None, :] + turn) % top, axis=1)


def shares(count, total, bound, skew, full):
    loads = [(1 << 20) // math.isqrt(standing ** skew) + 1 for standing in range(1, count + 1)]
    largest = bound if full else min(bound, max(-(-total // count), total * loads[0] // sum(loads)))
    least = 1 if total - largest >= count - 1 else 0
    given, spare = [largest] + [least] * (count - 1), total - largest - least * (count - 1)
    while spare > 0:
        candidates = [i for i in range(1, count) if given[i] < largest] or [i for i in range(1, count) if given[i] < bound]
        mass, budget = sum([loads[i] for i in candidates]), spare
        for i in candidates:
            more = min(bound - given[i], max(1, budget * loads[i] // mass), spare)
            given[i] = given[i] + more
            spare = spare - more
    return np.array(given)


def normal_values(key, dims, scale, most, cuts=(), kind=jnp.bfloat16):
    gain = block_levels(key, dims, cuts, -0.22, 0.18) if cuts else 1.0
    drawn = jax.random.normal(key, dims, jnp.float32) * scale * gain
    return jnp.minimum(jnp.maximum(drawn, -most), most).astype(kind)


def setup_inputs(seed: int = 0, part: int = 0) -> dict:
    streams_of = jax.random.split(jax.random.key(seed), 9)
    part_splits = jax.random.split(jax.random.fold_in(streams_of[8], part), 9)
    output_gradient = normal_values(part_splits[0], (TOKENS, EMBED_DIM), 0.25, 1.5, ((0, 4), (1, 4)))
    routes_keys = jax.random.split(jax.random.fold_in(part_splits[1], 1), TOKENS // TOK_DEV)
    routes_turns = jax.random.permutation(jax.random.fold_in(part_splits[1], 3), TOKENS // TOK_DEV)
    routes = jax.vmap(lambda own, number: assign_block(jax.random.fold_in(part_splits[1], 2), own, number, TOK_DEV, SPECIALIST_TOTAL, TOP, CAP, 2))(routes_keys, routes_turns).reshape((TOKENS, TOP))
    mixture_coefficients = jnp.clip(0.099609375 + 0.7988281 * jax.random.uniform(part_splits[2], (TOKENS, TOP), jnp.float32) ** block_levels(part_splits[2], (TOKENS, TOP), ((0, 4),), -0.2, 0.2), 0.099609375, 0.8984375).astype(jnp.bfloat16)
    gate_preactivation = normal_values(part_splits[3], (SPECIALIST_TOTAL, SLOTS, INNER_NEURONS), 1.0, 6.0, ((0, 4), (2, 4)))
    up_projection_saved = normal_values(part_splits[4], (SPECIALIST_TOTAL, SLOTS, INNER_NEURONS), 1.0, 6.0, ((0, 4), (2, 4)))
    down_matrix = normal_values(streams_of[5], (SPECIALIST_TOTAL, INNER_NEURONS, EMBED_DIM), INNER_NEURONS ** -0.5, 0.0625, ((0, 4), (1, 4)))
    lowrank_left_matrix = normal_values(streams_of[6], (SPECIALIST_TOTAL, LOWRANK_DIM, INNER_NEURONS), INNER_NEURONS ** -0.5, 0.0625, ((0, 4), (2, 4)))
    lowrank_right_matrix = normal_values(streams_of[7], (SPECIALIST_TOTAL, LOWRANK_DIM, EMBED_DIM), EMBED_DIM ** -0.5, 0.078125, ((0, 4),))
    return dict(output_gradient=output_gradient, routes=routes, mixture_coefficients=mixture_coefficients, gate_preactivation=gate_preactivation, up_projection_saved=up_projection_saved, down_matrix=down_matrix, lowrank_left_matrix=lowrank_left_matrix, lowrank_right_matrix=lowrank_right_matrix)


adapter_scale = 2.0


def positions(block):
    hot = (block[:, None] == jnp.arange(SPECIALIST_TOTAL, dtype=jnp.int32)[None, :]).astype(jnp.int32)
    before = jnp.cumsum(hot, axis=0) - hot
    return jnp.sum(before * hot, axis=1).astype(jnp.int32)


def single_expert(items):
    expert_rows, pick_e, gate_e, up_e, weight_e, first_expert_rows, second_e = items
    gate32 = gate_e.astype(jnp.float32)
    up32 = up_e.astype(jnp.float32)
    sigma = jax.nn.sigmoid(gate32)
    act = gate32 * sigma
    hidden = (act * up32).astype(jnp.bfloat16)
    rank_projection = jnp.dot(hidden, first_expert_rows.T, preferred_element_type=jnp.float32)
    backward_result = jnp.dot(expert_rows, second_e.T, preferred_element_type=jnp.float32).astype(jnp.bfloat16)
    hidden_gradient = jnp.dot(expert_rows, weight_e.T, preferred_element_type=jnp.float32)
    hidden_gradient = hidden_gradient + adapter_scale * jnp.dot(backward_result, first_expert_rows, preferred_element_type=jnp.float32)
    hidden_float = hidden.astype(jnp.float32)
    score = jnp.sum(hidden_float * hidden_gradient, axis=1)
    scaling_factor = pick_e.astype(jnp.float32)[:, None]
    scaled = scaling_factor * hidden_gradient
    gate_grad = (scaled * up32 * sigma * (1.0 + gate32 * (1.0 - sigma))).astype(jnp.bfloat16)
    up_grad = (scaled * act).astype(jnp.bfloat16)
    first_factor_gradient = adapter_scale * jnp.dot((scaling_factor * backward_result.astype(jnp.float32)).T, hidden_float, precision=lax.Precision.HIGHEST)
    second_factor_gradient = adapter_scale * jnp.dot((scaling_factor * rank_projection).T, expert_rows.astype(jnp.float32), precision=lax.Precision.HIGHEST)
    return gate_grad, up_grad, first_factor_gradient, second_factor_gradient, score


def reference(output_gradient, routes, mixture_coefficients, gate_preactivation, up_projection_saved, down_matrix, lowrank_left_matrix, lowrank_right_matrix):
    place = jax.vmap(positions)(routes.reshape(N_EXPERT, TOK_DEV * TOP))
    source = jnp.arange(N_EXPERT, dtype=jnp.int32)[:, None]
    slot = (source * CAP + place).reshape(-1).astype(jnp.int32)
    expert_ids = routes.reshape(-1)
    repeated = jnp.repeat(output_gradient, TOP, axis=0)
    token_rows = jnp.zeros((SPECIALIST_TOTAL, SLOTS, EMBED_DIM), jnp.bfloat16).at[expert_ids, slot].set(repeated)
    selected_slots = jnp.zeros((SPECIALIST_TOTAL, SLOTS), jnp.bfloat16).at[expert_ids, slot].set(mixture_coefficients.reshape(-1))
    gate_grad, up_grad, first_factor_gradient, second_factor_gradient, score = lax.map(
        single_expert, (token_rows, selected_slots, gate_preactivation, up_projection_saved, down_matrix, lowrank_left_matrix, lowrank_right_matrix))
    weight_grad = score[expert_ids, slot].reshape(TOKENS, TOP)
    return gate_grad, up_grad, first_factor_gradient, second_factor_gradient, weight_grad
```

```python
import jax
import jax.numpy as jnp
from jax import lax
from jax.sharding import PartitionSpec as P

CAP = 128


adapter_scale = 2.0


def positions(flat, count):
    hot = (flat[:, None] == jnp.arange(count, dtype=jnp.int32)[None, :]).astype(jnp.int32)
    before = jnp.cumsum(hot, axis=0) - hot
    return jnp.sum(before * hot, axis=1)


def contract_last(left, right):
    return lax.dot_general(
        left, right, (((1,), (1,)), ((), ())), preferred_element_type=jnp.float32
    )


def body(
    output_gradient,
    routes,
    mixture_coefficients,
    gate_preactivation,
    up_projection_saved,
    down_matrix,
    lowrank_left_matrix,
    lowrank_right_matrix,
):
    experts = lax.axis_size("expert")
    tok_rows = output_gradient.shape[0]
    slice_width = output_gradient.shape[1]
    flat = routes.reshape(-1)
    place = positions(flat, experts)
    key = (flat * CAP + place).reshape(tok_rows, 2)
    slots = jnp.arange(experts * CAP, dtype=jnp.int32)
    first = slots[:, None] == key[None, :, 0]
    second = slots[:, None] == key[None, :, 1]
    mix32 = mixture_coefficients.astype(jnp.float32)
    owner_pick = (
        jnp.sum(
            jnp.where(first, mix32[None, :, 0], 0.0) + jnp.where(second, mix32[None, :, 1], 0.0),
            axis=1,
        )
        .astype(jnp.bfloat16)
        .reshape(experts, CAP)
    )
    weight_local = down_matrix[0]
    second_factor_shard = lowrank_right_matrix[0]
    first_factor_shard = lowrank_left_matrix[0]
    buffer = jnp.dot(
        (first | second).astype(jnp.bfloat16),
        output_gradient,
        preferred_element_type=jnp.float32,
    ).astype(jnp.bfloat16).reshape(experts, CAP, slice_width)
    got_rows, got_pick = (
        lax.all_to_all(buffer, "expert", split_axis=0, concat_axis=0, tiled=True),
        lax.all_to_all(owner_pick, "expert", split_axis=0, concat_axis=0, tiled=True),
    )
    slice_rows = got_rows.reshape(experts * CAP, slice_width)
    selected_slots = got_pick.reshape(-1)
    piece = lax.all_gather(slice_rows, "mp", axis=1, tiled=True)
    base_gradient = contract_last(piece, weight_local)
    back32 = contract_last(piece, second_factor_shard)
    gate32 = gate_preactivation[0].astype(jnp.float32)
    up32 = up_projection_saved[0].astype(jnp.float32)
    sigma = jax.nn.sigmoid(gate32)
    act = gate32 * sigma
    hidden = (act * up32).astype(jnp.bfloat16)
    low_part = contract_last(hidden, first_factor_shard)
    backward_result = back32.astype(jnp.bfloat16)
    hidden_gradient = base_gradient + adapter_scale * jnp.dot(
        backward_result, first_factor_shard, preferred_element_type=jnp.float32
    )
    hidden_float = hidden.astype(jnp.float32)
    score_part = jnp.sum(hidden_float * hidden_gradient, axis=1)
    rank_projection, score = lax.psum((low_part, score_part), "mp")
    scaling_factor = selected_slots.astype(jnp.float32)[:, None]
    scaled = scaling_factor * hidden_gradient
    gate_grad = (scaled * up32 * sigma * (1.0 + gate32 * (1.0 - sigma))).astype(jnp.bfloat16)
    up_grad = (scaled * act).astype(jnp.bfloat16)
    first_factor_gradient = adapter_scale * jnp.dot(
        (scaling_factor * backward_result.astype(jnp.float32)).T,
        hidden_float,
        precision=lax.Precision.HIGHEST,
    )
    second_factor_gradient = adapter_scale * jnp.dot(
        (scaling_factor * rank_projection).T,
        slice_rows.astype(jnp.float32),
        precision=lax.Precision.HIGHEST,
    )
    returned = lax.all_to_all(
        score.reshape(experts, CAP), "expert", split_axis=0, concat_axis=0, tiled=True
    )
    returned_flat = returned.reshape(1, -1)
    weight_grad = jnp.stack(
        [
            jnp.sum(jnp.where(key[:, k : k + 1] == slots[None, :], returned_flat, 0.0), axis=1)
            for k in range(2)
        ],
        axis=1,
    )
    return (
        gate_grad[None],
        up_grad[None],
        first_factor_gradient[None],
        second_factor_gradient[None],
        weight_grad,
    )


def solution(mesh):
    placed = (
        P(("groups", "expert"), "mp"),
        P(("groups", "expert"), None),
        P(("groups", "expert"), None),
        P("expert", "groups", "mp"),
        P("expert", "groups", "mp"),
        P("expert", "mp", None),
        P("expert", None, "mp"),
        P("expert", None, None),
    )
    return jax.shard_map(
        body,
        mesh=mesh,
        in_specs=placed,
        out_specs=(
            P("expert", "groups", "mp"),
            P("expert", "groups", "mp"),
            P(("groups", "expert"), None, "mp"),
            P(("groups", "expert"), None, "mp"),
            P(("groups", "expert"), None),
        ),
        check_vma=False,
    )
```

```python
import functools

import jax
import jax.numpy as jnp
from jax import lax
from jax.experimental import pallas as pl
from jax.experimental.pallas import tpu as pltpu
from jax.sharding import PartitionSpec as P

CAP = 128
TILE = 256
LAG = 2
WBUFS = 4
MESH = pl.DeviceIdType.MESH

adapter_scale = 2.0


def positions(flat, count):
    hot = (flat[:, None] == jnp.arange(count, dtype=jnp.int32)[None, :]).astype(jnp.int32)
    before = jnp.cumsum(hot, axis=0) - hot
    return jnp.sum(before * hot, axis=1)


def contract_last(left, right):
    return lax.dot_general(
        left, right, (((1,), (1,)), ((), ())), preferred_element_type=jnp.float32
    )


def split_dot(left, right):
    high = left.astype(jnp.bfloat16)
    low = (left - high.astype(jnp.float32)).astype(jnp.bfloat16)
    return jnp.dot(high, right, preferred_element_type=jnp.float32) + jnp.dot(
        low, right, preferred_element_type=jnp.float32
    )


def turned(row, count):
    return jnp.transpose(jnp.broadcast_to(row, (count, row.shape[1])))


def kernel(
    n_z, n_e, halves,
    tok, meta, gate, up, weight, left_m, right_m,
    gate_out, up_out, a_out, b_out, w_out,
    tbuf, wbuf, dh, hid, coef, act, gbuf, ubuf, rows, own_rows, dmat, metas,
    pick_col, pick_row, back_t, low_acc, low_all, score_all, score_back, score_acc,
    load_sem, w_sem, io_sem, out_sem, zrecv, zright, zleft, xsend, xrecv, ssend, srecv,
    msend, mrecv, lsend, lrecv, csend, crecv, dsend, drecv,
):
    me = lax.axis_index("expert")
    z = lax.axis_index("mp")
    n_x = n_e // 2
    x, core = me // 2, me % 2
    width = tok.shape[1] // halves
    items = n_z * halves
    hidden_units = gate.shape[1]
    tiles = hidden_units // TILE

    def remote(src, dst, send, recv, where):
        return pltpu.make_async_remote_copy(
            src_ref=src, dst_ref=dst, send_sem=send, recv_sem=recv,
            device_id=where, device_id_type=MESH,
        )

    def zcopy(chunk, to, send):
        block = tbuf.at[chunk, me]
        return remote(block, block, send.at[chunk], zrecv.at[chunk], {"mp": to})

    def xcopy(chunk, k):
        block = tbuf.at[chunk, me]
        to = ((x + k) % n_x) * 2 + core
        return remote(block, block, xsend.at[k - 1, chunk], xrecv.at[k - 1, chunk], {"expert": to})

    def xarrival(chunk, k):
        block = tbuf.at[chunk, ((x + n_x - k) % n_x) * 2 + core]
        to = ((x + k) % n_x) * 2 + core
        return remote(block, block, xsend.at[k - 1, chunk], xrecv.at[k - 1, chunk], {"expert": to})

    def scopy(chunk, xs):
        block = tbuf.at[chunk, xs * 2 + core]
        return remote(block, block, ssend.at[xs, chunk], srecv.at[xs, chunk], {"expert": x * 2 + 1 - core})

    def sarrival(chunk, xs):
        block = tbuf.at[chunk, xs * 2 + 1 - core]
        return remote(block, block, ssend.at[xs, chunk], srecv.at[xs, chunk], {"expert": x * 2 + 1 - core})

    def spread(chunk):
        for k in range(1, n_x):
            xcopy(chunk, k).start()
        scopy(chunk, x).start()

    def item_chunk(i):
        j, h = i // halves, i % halves
        m = jnp.minimum(z, n_z - 1 - z)
        near = jnp.where(j % 2 == 1, z - (j + 1) // 2, z + j // 2)
        far = jnp.where(z > n_z - 1 - z, z - (j - m), z + (j - m))
        return jnp.where(j <= 2 * m, near, far) * halves + h

    def load(h):
        return pltpu.make_async_copy(
            tok.at[:, pl.ds(h * width, width)], tbuf.at[z * halves + h, me], load_sem.at[h]
        )

    def wload(i):
        chunk = item_chunk(i)
        return pltpu.make_async_copy(
            weight.at[:, pl.ds(pl.multiple_of(chunk * width, 128), width)],
            wbuf.at[i % WBUFS],
            w_sem.at[i % WBUFS],
        )

    for h in range(halves):
        load(h).start()
    gate_in = pltpu.make_async_copy(gate, gbuf, io_sem.at[0])
    up_in = pltpu.make_async_copy(up, ubuf, io_sem.at[1])
    gate_in.start()
    up_in.start()

    barrier = pltpu.get_barrier_semaphore()
    for k in range(1, n_e):
        pl.semaphore_signal(barrier, inc=1, device_id={"expert": (me + k) % n_e}, device_id_type=MESH)
    for k in range(1, n_z):
        pl.semaphore_signal(barrier, inc=1, device_id={"mp": (z + k) % n_z}, device_id_type=MESH)
    pl.semaphore_wait(barrier, n_e + n_z - 2)

    def mcopy(k):
        return remote(meta, metas.at[me], msend.at[k - 1], mrecv.at[k - 1], {"expert": (me + k) % n_e})

    def marrival(k):
        return remote(
            meta, metas.at[(me + n_e - k) % n_e], msend.at[k - 1], mrecv.at[k - 1],
            {"expert": (me + k) % n_e},
        )

    for k in range(1, n_e):
        mcopy(k).start()
    for h in range(halves):
        chunk = z * halves + h
        load(h).wait()

        @pl.when(z < n_z - 1)
        def _():
            zcopy(chunk, z + 1, zright).start()

        @pl.when(z > 0)
        def _():
            zcopy(chunk, z - 1, zleft).start()

        spread(chunk)
    for i in range(WBUFS):
        wload(i).start()
    metas[pl.ds(me, 1)] = meta[...][None]
    low_acc[...] = jnp.zeros_like(low_acc)
    back_t[...] = jnp.zeros_like(back_t)
    for k in range(1, n_e):
        marrival(k).wait_recv()
    tokens = meta.shape[1]
    slot = lax.broadcasted_iota(jnp.int32, (CAP, tokens), 0)

    def masks(keys, base):
        numbers = (slot + base).astype(jnp.float32)
        return numbers == keys[0:1, :], numbers == keys[1:2, :]

    for o in range(n_e):
        keys = metas[o]
        first, second = masks(keys, me * CAP)
        dmat[o] = (jnp.where(first, 1.0, 0.0) + jnp.where(second, 1.0, 0.0)).astype(jnp.bfloat16)
        col = jnp.sum(
            jnp.where(first, keys[2:3, :], 0.0) + jnp.where(second, keys[3:4, :], 0.0),
            axis=1, keepdims=True,
        )
        wide = jnp.broadcast_to(col, (CAP, 128))
        pick_col[o * CAP:(o + 1) * CAP, :] = wide
        pick_row[:, o * CAP:(o + 1) * CAP] = jnp.transpose(wide)[0:8, :]
    gate_in.wait()
    up_in.wait()

    def lcopy(k):
        return remote(low_acc, low_all.at[z], lsend.at[k - 1], lrecv.at[k - 1], {"mp": (z + k) % n_z})

    def larrival(k):
        return remote(
            low_acc, low_all.at[(z + n_z - k) % n_z], lsend.at[k - 1], lrecv.at[k - 1],
            {"mp": (z + k) % n_z},
        )

    def prepare(n):
        cols = pl.ds(pl.multiple_of(n * TILE, TILE), TILE)
        g = gbuf[:, cols].astype(jnp.float32)
        u = ubuf[:, cols].astype(jnp.float32)
        sigma = jax.nn.sigmoid(g)
        a = g * sigma
        hidden = (a * u).astype(jnp.bfloat16)
        hid[:, cols] = hidden
        act[:, cols] = a
        coef[:, cols] = u * sigma * (1.0 + g * (1.0 - sigma))
        dh[:, cols] = jnp.zeros((dh.shape[0], TILE), jnp.float32)
        low_acc[...] += contract_last(left_m[:, cols], hidden)

    per_step = -(-tiles // LAG)

    def product(i):
        chunk = item_chunk(i)
        for k in range(1, n_x):
            xarrival(chunk, k).wait_recv()
            scopy(chunk, (x + n_x - k) % n_x).start()
        for k in range(n_x):
            sarrival(chunk, (x + n_x - k) % n_x).wait_recv()
        for o in range(n_e):
            rows[o * CAP:(o + 1) * CAP, :] = jnp.dot(
                dmat[o], tbuf[chunk, o], preferred_element_type=jnp.float32
            ).astype(jnp.bfloat16)

        @pl.when(i < halves)
        def _():
            own_rows[i % halves] = rows[...]

        back_t[...] += contract_last(
            right_m[:, pl.ds(pl.multiple_of(chunk * width, 128), width)], rows[...]
        )
        wload(i).wait()

        def tile(n, carry):
            at = pl.ds(pl.multiple_of(n * TILE, TILE), TILE)
            dh[:, at] += contract_last(rows[...], wbuf[i % WBUFS, at, :])
            return carry

        lax.fori_loop(0, tiles, tile, 0)

        @pl.when(i + WBUFS < items)
        def _():
            wload(i + WBUFS).start()

    def step(t, carry):
        @pl.when((t >= halves) & (t < items))
        def _():
            d, h = t // halves, t % halves

            @pl.when(z - d >= 0)
            def _():
                chunk = (z - d) * halves + h
                zcopy(chunk, z, zright).wait_recv()

                @pl.when(z < n_z - 1)
                def _():
                    zcopy(chunk, z + 1, zright).start()

                spread(chunk)

            @pl.when(z + d < n_z)
            def _():
                chunk = (z + d) * halves + h
                zcopy(chunk, z, zleft).wait_recv()

                @pl.when(z > 0)
                def _():
                    zcopy(chunk, z - 1, zleft).start()

                spread(chunk)

        @pl.when(t < LAG)
        def _():
            def some(n, carry):
                prepare(n)
                return carry

            lax.fori_loop(t * per_step, jnp.minimum((t + 1) * per_step, tiles), some, 0)

        @pl.when(t >= LAG)
        def _():
            product(t - LAG)

        return carry

    lax.fori_loop(0, LAG, step, 0)
    low_all[pl.ds(z, 1)] = low_acc[...][None]
    for k in range(1, n_z):
        lcopy(k).start()
    lax.fori_loop(LAG, items + LAG, step, 0)

    back = back_t[...].astype(jnp.bfloat16).astype(jnp.float32)
    back_col = jnp.transpose(back).astype(jnp.bfloat16)
    score_acc[...] = jnp.zeros_like(score_acc)

    def outs(n):
        cols = pl.ds(pl.multiple_of(n * TILE, TILE), TILE)
        return (
            pltpu.make_async_copy(gbuf.at[:, cols], gate_out.at[:, cols], out_sem.at[0, n]),
            pltpu.make_async_copy(ubuf.at[:, cols], up_out.at[:, cols], out_sem.at[1, n]),
        )

    def finish(n, carry):
        cols = pl.ds(pl.multiple_of(n * TILE, TILE), TILE)
        d = dh[:, cols] + adapter_scale * jnp.dot(
            back_col, left_m[:, cols], preferred_element_type=jnp.float32
        )
        prod = hid[:, cols].astype(jnp.float32) * d
        total = prod[:, 0:128]
        for q in range(1, TILE // 128):
            total = total + prod[:, q * 128:(q + 1) * 128]
        score_acc[...] += total
        scaled = pick_col[:, 0:1] * d
        gbuf[:, cols] = (scaled * coef[:, cols]).astype(jnp.bfloat16)
        ubuf[:, cols] = (scaled * act[:, cols]).astype(jnp.bfloat16)
        for copy in outs(n):
            copy.start()
        return carry

    lax.fori_loop(0, tiles, finish, 0)

    mine = jnp.sum(jnp.transpose(score_acc[...]), axis=0, keepdims=True)
    score_all[pl.ds(z, 1)] = jnp.broadcast_to(mine, (8, mine.shape[1]))[None]

    def ccopy(k):
        block = score_all.at[z]
        return remote(block, block, csend.at[k - 1], crecv.at[k - 1], {"mp": (z + k) % n_z})

    def carrival(k):
        block = score_all.at[(z + n_z - k) % n_z]
        return remote(block, block, csend.at[k - 1], crecv.at[k - 1], {"mp": (z + k) % n_z})

    for k in range(1, n_z):
        ccopy(k).start()

    a_out[...] = adapter_scale * split_dot(pick_row[0:1, :] * back, hid[...])

    for k in range(1, n_z):
        carrival(k).wait_recv()
    whole = score_all[0]
    for k in range(1, n_z):
        whole = whole + score_all[k]
    for o in range(n_e):
        score_back[0, o] = whole[:, o * CAP:(o + 1) * CAP]

    def dcopy(k):
        to = (me + k) % n_e
        return remote(
            score_back.at[0, to], score_back.at[1, me], dsend.at[k - 1], drecv.at[k - 1], {"expert": to}
        )

    def darrival(k):
        return remote(
            score_back.at[0, (me + k) % n_e], score_back.at[1, (me + n_e - k) % n_e],
            dsend.at[k - 1], drecv.at[k - 1], {"expert": (me + k) % n_e},
        )

    for k in range(1, n_e):
        dcopy(k).start()
    score_back[1, pl.ds(me, 1)] = score_back[0, pl.ds(me, 1)]

    for k in range(1, n_z):
        larrival(k).wait_recv()
    low = low_all[0]
    for k in range(1, n_z):
        low = low + low_all[k]
    low = pick_row[0:1, :] * low
    for h in range(halves):
        b_out[:, h * width:(h + 1) * width] = adapter_scale * split_dot(low, own_rows[h])

    for k in range(1, n_e):
        darrival(k).wait_recv()
    firsts = jnp.zeros((1, tokens), jnp.float32)
    seconds = jnp.zeros((1, tokens), jnp.float32)
    for o in range(n_e):
        first, second = masks(meta[...], o * CAP)
        col = turned(score_back[1, o][0:1, :], CAP)[:, 0:1]
        firsts = firsts + jnp.sum(jnp.where(first, col, 0.0), axis=0, keepdims=True)
        seconds = seconds + jnp.sum(jnp.where(second, col, 0.0), axis=0, keepdims=True)
    w_out[0:1, :] = firsts
    w_out[1:2, :] = seconds

    def drain(chunk, carry):
        zs = chunk // halves

        @pl.when((zs <= z) & (z < n_z - 1))
        def _():
            zcopy(chunk, z + 1, zright).wait_send()

        @pl.when((zs >= z) & (z > 0))
        def _():
            zcopy(chunk, z - 1, zleft).wait_send()

        for k in range(1, n_x):
            xcopy(chunk, k).wait_send()
        for k in range(n_x):
            scopy(chunk, (x + k) % n_x).wait_send()
        return carry

    lax.fori_loop(0, items, drain, 0)
    for k in range(1, n_e):
        mcopy(k).wait_send()
        dcopy(k).wait_send()
    for k in range(1, n_z):
        lcopy(k).wait_send()
        ccopy(k).wait_send()

    def flush(n, carry):
        for copy in outs(n):
            copy.wait()
        return carry

    lax.fori_loop(0, tiles, flush, 0)


def body(
    output_gradient,
    routes,
    mixture_coefficients,
    gate_preactivation,
    up_projection_saved,
    down_matrix,
    lowrank_left_matrix,
    lowrank_right_matrix,
):
    n_e = lax.axis_size("expert")
    n_z = lax.axis_size("mp")
    tokens, span = output_gradient.shape
    halves = 2 if span % 256 == 0 else 1
    width = span // halves
    items = n_z * halves
    n_x = n_e // 2
    slots, units = gate_preactivation.shape[1:]
    rank = lowrank_left_matrix.shape[1]
    model = down_matrix.shape[2]
    tiles = units // TILE

    flat = routes.reshape(-1)
    key = (flat * CAP + positions(flat, n_e)).reshape(tokens, 2)
    meta = jnp.concatenate(
        [key.astype(jnp.float32).T, mixture_coefficients.astype(jnp.float32).T,
         jnp.zeros((4, tokens), jnp.float32)], axis=0
    )
    bf, f32 = jnp.bfloat16, jnp.float32
    anywhere = pl.BlockSpec(memory_space=pl.ANY)
    vmem = pl.BlockSpec(memory_space=pltpu.VMEM)
    dma = pltpu.SemaphoreType.DMA
    gate_grad, up_grad, a_grad, b_grad, scores = pl.pallas_call(
        functools.partial(kernel, n_z, n_e, halves),
        out_shape=(
            jax.ShapeDtypeStruct((slots, units), bf),
            jax.ShapeDtypeStruct((slots, units), bf),
            jax.ShapeDtypeStruct((rank, units), f32),
            jax.ShapeDtypeStruct((rank, span), f32),
            jax.ShapeDtypeStruct((2, tokens), f32),
        ),
        in_specs=[anywhere, vmem, anywhere, anywhere, anywhere, vmem, vmem],
        out_specs=(anywhere, anywhere, vmem, vmem, vmem),
        scratch_shapes=[
            pltpu.VMEM((items, n_e, tokens, width), bf),
            pltpu.VMEM((WBUFS, units, width), bf),
            pltpu.VMEM((slots, units), f32),
            pltpu.VMEM((slots, units), bf),
            pltpu.VMEM((slots, units), f32),
            pltpu.VMEM((slots, units), f32),
            pltpu.VMEM((slots, units), bf),
            pltpu.VMEM((slots, units), bf),
            pltpu.VMEM((slots, width), bf),
            pltpu.VMEM((halves, slots, width), bf),
            pltpu.VMEM((n_e, CAP, tokens), bf),
            pltpu.VMEM((n_e, 8, tokens), f32),
            pltpu.VMEM((slots, 128), f32),
            pltpu.VMEM((8, slots), f32),
            pltpu.VMEM((rank, slots), f32),
            pltpu.VMEM((rank, slots), f32),
            pltpu.VMEM((n_z, rank, slots), f32),
            pltpu.VMEM((n_z, 8, slots), f32),
            pltpu.VMEM((2, n_e, 8, CAP), f32),
            pltpu.VMEM((slots, 128), f32),
            dma((halves,)),
            dma((WBUFS,)),
            dma((2,)),
            dma((2, tiles)),
            dma((items,)),
            dma((items,)),
            dma((items,)),
            dma((n_x - 1, items)),
            dma((n_x - 1, items)),
            dma((n_x, items)),
            dma((n_x, items)),
            dma((n_e - 1,)),
            dma((n_e - 1,)),
            dma((n_z - 1,)),
            dma((n_z - 1,)),
            dma((n_z - 1,)),
            dma((n_z - 1,)),
            dma((n_e - 1,)),
            dma((n_e - 1,)),
        ],
        compiler_params=pltpu.CompilerParams(
            collective_id=0, has_side_effects=True, vmem_limit_bytes=60 * 1024 * 1024
        ),
        cost_estimate=pl.CostEstimate(
            flops=2 * slots * units * model,
            bytes_accessed=2 * units * model,
            transcendentals=slots * units,
        ),
    )(
        output_gradient, meta, gate_preactivation[0], up_projection_saved[0],
        down_matrix[0], lowrank_left_matrix[0], lowrank_right_matrix[0],
    )
    return gate_grad[None], up_grad[None], a_grad[None], b_grad[None], scores.T


def solution(mesh):
    placed = (
        P(("groups", "expert"), "mp"),
        P(("groups", "expert"), None),
        P(("groups", "expert"), None),
        P("expert", "groups", "mp"),
        P("expert", "groups", "mp"),
        P("expert", "mp", None),
        P("expert", None, "mp"),
        P("expert", None, None),
    )
    return jax.shard_map(
        body,
        mesh=mesh,
        in_specs=placed,
        out_specs=(
            P("expert", "groups", "mp"),
            P("expert", "groups", "mp"),
            P(("groups", "expert"), None, "mp"),
            P(("groups", "expert"), None, "mp"),
            P(("groups", "expert"), None),
        ),
        check_vma=False,
    )
```

```python
import functools

import jax
import jax.numpy as jnp
from jax import lax
from jax.experimental import pallas as pl
from jax.experimental.pallas import tpu as pltpu
from jax.sharding import PartitionSpec as P

CAP = 128
TILE = 256
LAG = 2
WBUFS = 4
MESH = pl.DeviceIdType.MESH

adapter_scale = 2.0


def contract_last(left, right):
    return lax.dot_general(
        left, right, (((1,), (1,)), ((), ())), preferred_element_type=jnp.float32
    )


def split_dot(left, right):
    high = left.astype(jnp.bfloat16)
    low = (left - high.astype(jnp.float32)).astype(jnp.bfloat16)
    return jnp.dot(high, right, preferred_element_type=jnp.float32) + jnp.dot(
        low, right, preferred_element_type=jnp.float32
    )


def turned(row, count):
    return jnp.transpose(jnp.broadcast_to(row, (count, row.shape[1])))


def kernel(
    n_z, n_e, halves,
    tok, routes, mix, gate, up, weight, left_m, right_m,
    gate_out, up_out, a_out, b_out, w_out,
    tbuf, wbuf, dh, hid, coef, act, gbuf, ubuf, rows, own_rows, dmat, meta, metas,
    pick_col, pick_row, back_t, low_acc, low_all, score_all, score_back, score_acc,
    load_sem, w_sem, io_sem, out_sem, zrecv, zright, zleft, xsend, xrecv, ssend, srecv,
    psend, precv, msend, mrecv, lsend, lrecv, csend, crecv, dsend, drecv,
):
    me = lax.axis_index("expert")
    z = lax.axis_index("mp")
    n_x = n_e // 2
    x, core = me // 2, me % 2
    width = tok.shape[1] // halves
    items = n_z * halves
    hidden_units = gate.shape[1]
    tiles = hidden_units // TILE
    detour = n_x == 2 and halves == 2 and n_z % 2 == 0
    pair = z + 1 - 2 * (z % 2)
    late_at = jnp.where((z % 2 == 1) | (z == 0), 3, 5)

    def remote(src, dst, send, recv, where):
        return pltpu.make_async_remote_copy(
            src_ref=src, dst_ref=dst, send_sem=send, recv_sem=recv,
            device_id=where, device_id_type=MESH,
        )

    def zcopy(chunk, to, send):
        block = tbuf.at[chunk, me]
        return remote(block, block, send.at[chunk], zrecv.at[chunk], {"mp": to})

    def xcopy(chunk, k):
        block = tbuf.at[chunk, me]
        to = ((x + k) % n_x) * 2 + core
        return remote(block, block, xsend.at[k - 1, chunk], xrecv.at[k - 1, chunk], {"expert": to})

    def xarrival(chunk, k):
        block = tbuf.at[chunk, ((x + n_x - k) % n_x) * 2 + core]
        to = ((x + k) % n_x) * 2 + core
        return remote(block, block, xsend.at[k - 1, chunk], xrecv.at[k - 1, chunk], {"expert": to})

    def scopy(chunk, xs):
        block = tbuf.at[chunk, xs * 2 + core]
        return remote(block, block, ssend.at[xs, chunk], srecv.at[xs, chunk], {"expert": x * 2 + 1 - core})

    def sarrival(chunk, xs):
        block = tbuf.at[chunk, xs * 2 + 1 - core]
        return remote(block, block, ssend.at[xs, chunk], srecv.at[xs, chunk], {"expert": x * 2 + 1 - core})

    def direct(chunk):
        return (chunk != pair * halves + 1) if detour else (chunk >= 0)

    def pcopy():
        block = tbuf.at[z * halves + 1, (1 - x) * 2 + core]
        return remote(block, block, psend.at[0], precv.at[0], {"mp": pair})

    def parrival():
        block = tbuf.at[pair * halves + 1, (1 - x) * 2 + core]
        return remote(block, block, psend.at[0], precv.at[0], {"mp": pair})

    def spread(chunk):
        @pl.when(direct(chunk))
        def _():
            for k in range(1, n_x):
                xcopy(chunk, k).start()

        scopy(chunk, x).start()

    def item_chunk(i):
        if detour:
            i = jnp.where(i < late_at, i, jnp.where(i == items - 1, late_at, i + 1))
        j, h = i // halves, i % halves
        m = jnp.minimum(z, n_z - 1 - z)
        near = jnp.where(j % 2 == 1, z - (j + 1) // 2, z + j // 2)
        far = jnp.where(z > n_z - 1 - z, z - (j - m), z + (j - m))
        return jnp.where(j <= 2 * m, near, far) * halves + h

    def load(h):
        return pltpu.make_async_copy(
            tok.at[:, pl.ds(h * width, width)], tbuf.at[z * halves + h, me], load_sem.at[h]
        )

    def wload(i):
        chunk = item_chunk(i)
        return pltpu.make_async_copy(
            weight.at[:, pl.ds(pl.multiple_of(chunk * width, 128), width)],
            wbuf.at[i % WBUFS],
            w_sem.at[i % WBUFS],
        )

    for h in range(halves):
        load(h).start()
    gate_in = pltpu.make_async_copy(gate, gbuf, io_sem.at[0])
    up_in = pltpu.make_async_copy(up, ubuf, io_sem.at[1])
    gate_in.start()
    up_in.start()

    barrier = pltpu.get_barrier_semaphore()
    for k in range(1, n_e):
        pl.semaphore_signal(barrier, inc=1, device_id={"expert": (me + k) % n_e}, device_id_type=MESH)
    for k in range(1, n_z):
        pl.semaphore_signal(barrier, inc=1, device_id={"mp": (z + k) % n_z}, device_id_type=MESH)
    pl.semaphore_wait(barrier, n_e + n_z - 2)

    def mcopy(k):
        return remote(meta, metas.at[me], msend.at[k - 1], mrecv.at[k - 1], {"expert": (me + k) % n_e})

    def marrival(k):
        return remote(
            meta, metas.at[(me + n_e - k) % n_e], msend.at[k - 1], mrecv.at[k - 1],
            {"expert": (me + k) % n_e},
        )

    for h in range(halves):
        chunk = z * halves + h
        load(h).wait()

        @pl.when(z < n_z - 1)
        def _():
            zcopy(chunk, z + 1, zright).start()

        @pl.when(z > 0)
        def _():
            zcopy(chunk, z - 1, zleft).start()

        spread(chunk)
    for i in range(WBUFS):
        wload(i).start()
    tokens = routes.shape[1]
    named = routes[...].astype(jnp.float32)
    wanted = lax.broadcasted_iota(jnp.int32, (16, tokens), 0).astype(jnp.float32)
    hot = jnp.where(wanted == named[0:1, :], 1.0, 0.0) + jnp.where(wanted == named[1:2, :], 1.0, 0.0)
    earlier = (
        lax.broadcasted_iota(jnp.int32, (tokens, tokens), 0)
        < lax.broadcasted_iota(jnp.int32, (tokens, tokens), 1)
    )
    before = jnp.dot(
        hot.astype(jnp.bfloat16),
        jnp.where(earlier, 1.0, 0.0).astype(jnp.bfloat16),
        preferred_element_type=jnp.float32,
    )
    meta[...] = jnp.zeros_like(meta)
    for k in range(2):
        one = named[k:k + 1, :]
        place = jnp.sum(jnp.where(wanted == one, before, 0.0), axis=0, keepdims=True)
        meta[k:k + 1, :] = one * CAP + place
    meta[2:4, :] = mix[...].astype(jnp.float32)
    for k in range(1, n_e):
        mcopy(k).start()
    metas[pl.ds(me, 1)] = meta[...][None]
    low_acc[...] = jnp.zeros_like(low_acc)
    back_t[...] = jnp.zeros_like(back_t)
    for k in range(1, n_e):
        marrival(k).wait_recv()
    slot = lax.broadcasted_iota(jnp.int32, (CAP, tokens), 0)

    def masks(keys, base):
        numbers = (slot + base).astype(jnp.float32)
        return numbers == keys[0:1, :], numbers == keys[1:2, :]

    for o in range(n_e):
        keys = metas[o]
        first, second = masks(keys, me * CAP)
        dmat[o] = (jnp.where(first, 1.0, 0.0) + jnp.where(second, 1.0, 0.0)).astype(jnp.bfloat16)
        col = jnp.sum(
            jnp.where(first, keys[2:3, :], 0.0) + jnp.where(second, keys[3:4, :], 0.0),
            axis=1, keepdims=True,
        )
        wide = jnp.broadcast_to(col, (CAP, 128))
        pick_col[o * CAP:(o + 1) * CAP, :] = wide
        pick_row[:, o * CAP:(o + 1) * CAP] = jnp.transpose(wide)[0:8, :]
    gate_in.wait()
    up_in.wait()

    def lcopy(k):
        return remote(low_acc, low_all.at[z], lsend.at[k - 1], lrecv.at[k - 1], {"mp": (z + k) % n_z})

    def larrival(k):
        return remote(
            low_acc, low_all.at[(z + n_z - k) % n_z], lsend.at[k - 1], lrecv.at[k - 1],
            {"mp": (z + k) % n_z},
        )

    def prepare(n):
        cols = pl.ds(pl.multiple_of(n * TILE, TILE), TILE)
        g = gbuf[:, cols].astype(jnp.float32)
        u = ubuf[:, cols].astype(jnp.float32)
        sigma = jax.nn.sigmoid(g)
        a = g * sigma
        hidden = (a * u).astype(jnp.bfloat16)
        hid[:, cols] = hidden
        act[:, cols] = a
        coef[:, cols] = u * sigma * (1.0 + g * (1.0 - sigma))
        dh[:, cols] = jnp.zeros((dh.shape[0], TILE), jnp.float32)
        low_acc[...] += contract_last(left_m[:, cols], hidden)

    per_step = -(-tiles // LAG)

    def product(i):
        chunk = item_chunk(i)
        @pl.when(direct(chunk))
        def _():
            for k in range(1, n_x):
                xarrival(chunk, k).wait_recv()

        if detour:
            @pl.when(chunk == pair * halves + 1)
            def _():
                parrival().wait_recv()

        for k in range(1, n_x):
            scopy(chunk, (x + n_x - k) % n_x).start()
        for k in range(n_x):
            sarrival(chunk, (x + n_x - k) % n_x).wait_recv()
        for o in range(n_e):
            rows[o * CAP:(o + 1) * CAP, :] = jnp.dot(
                dmat[o], tbuf[chunk, o], preferred_element_type=jnp.float32
            ).astype(jnp.bfloat16)

        @pl.when(i < halves)
        def _():
            own_rows[i % halves] = rows[...]

        back_t[...] += contract_last(
            right_m[:, pl.ds(pl.multiple_of(chunk * width, 128), width)], rows[...]
        )
        wload(i).wait()

        def tile(n, carry):
            at = pl.ds(pl.multiple_of(n * TILE, TILE), TILE)
            dh[:, at] += contract_last(rows[...], wbuf[i % WBUFS, at, :])
            return carry

        lax.fori_loop(0, tiles, tile, 0)

        @pl.when(i + WBUFS < items)
        def _():
            wload(i + WBUFS).start()

    def step(t, carry):
        @pl.when((t >= halves) & (t < items))
        def _():
            d, h = t // halves, t % halves

            @pl.when(z - d >= 0)
            def _():
                chunk = (z - d) * halves + h
                zcopy(chunk, z, zright).wait_recv()

                @pl.when(z < n_z - 1)
                def _():
                    zcopy(chunk, z + 1, zright).start()

                spread(chunk)

            @pl.when(z + d < n_z)
            def _():
                chunk = (z + d) * halves + h
                zcopy(chunk, z, zleft).wait_recv()

                @pl.when(z > 0)
                def _():
                    zcopy(chunk, z - 1, zleft).start()

                spread(chunk)

        if detour:
            @pl.when(t == items - halves - 1)
            def _():
                pcopy().start()

        @pl.when(t < LAG)
        def _():
            def some(n, carry):
                prepare(n)
                return carry

            lax.fori_loop(t * per_step, jnp.minimum((t + 1) * per_step, tiles), some, 0)

        @pl.when(t >= LAG)
        def _():
            product(t - LAG)

        return carry

    lax.fori_loop(0, LAG, step, 0)
    low_all[pl.ds(z, 1)] = low_acc[...][None]
    for k in range(1, n_z):
        lcopy(k).start()
    lax.fori_loop(LAG, items + LAG, step, 0)

    back = back_t[...].astype(jnp.bfloat16).astype(jnp.float32)
    back_col = (adapter_scale * jnp.transpose(back)).astype(jnp.bfloat16)
    pick = jnp.concatenate([pick_col[...]] * (TILE // 128), axis=1)
    score_acc[...] = jnp.zeros_like(score_acc)

    def outs(n):
        cols = pl.ds(pl.multiple_of(n * TILE, TILE), TILE)
        return (
            pltpu.make_async_copy(gbuf.at[:, cols], gate_out.at[:, cols], out_sem.at[0, n]),
            pltpu.make_async_copy(ubuf.at[:, cols], up_out.at[:, cols], out_sem.at[1, n]),
        )

    def finish(n, carry):
        cols = pl.ds(pl.multiple_of(n * TILE, TILE), TILE)
        d = dh[:, cols] + jnp.dot(
            back_col, left_m[:, cols], preferred_element_type=jnp.float32
        )
        prod = hid[:, cols].astype(jnp.float32) * d
        total = prod[:, 0:128]
        for q in range(1, TILE // 128):
            total = total + prod[:, q * 128:(q + 1) * 128]
        score_acc[...] += total
        scaled = pick * d
        gbuf[:, cols] = (scaled * coef[:, cols]).astype(jnp.bfloat16)
        ubuf[:, cols] = (scaled * act[:, cols]).astype(jnp.bfloat16)
        for copy in outs(n):
            copy.start()
        return carry

    lax.fori_loop(0, tiles, finish, 0)

    mine = jnp.sum(jnp.transpose(score_acc[...]), axis=0, keepdims=True)
    score_all[pl.ds(z, 1)] = jnp.broadcast_to(mine, (8, mine.shape[1]))[None]

    def ccopy(k):
        block = score_all.at[z]
        return remote(block, block, csend.at[k - 1], crecv.at[k - 1], {"mp": (z + k) % n_z})

    def carrival(k):
        block = score_all.at[(z + n_z - k) % n_z]
        return remote(block, block, csend.at[k - 1], crecv.at[k - 1], {"mp": (z + k) % n_z})

    for k in range(1, n_z):
        ccopy(k).start()

    a_out[...] = adapter_scale * split_dot(pick_row[0:1, :] * back, hid[...])

    for k in range(1, n_z):
        carrival(k).wait_recv()
    whole = score_all[0]
    for k in range(1, n_z):
        whole = whole + score_all[k]
    for o in range(n_e):
        score_back[0, o] = whole[:, o * CAP:(o + 1) * CAP]

    def dcopy(k):
        to = (me + k) % n_e
        return remote(
            score_back.at[0, to], score_back.at[1, me], dsend.at[k - 1], drecv.at[k - 1], {"expert": to}
        )

    def darrival(k):
        return remote(
            score_back.at[0, (me + k) % n_e], score_back.at[1, (me + n_e - k) % n_e],
            dsend.at[k - 1], drecv.at[k - 1], {"expert": (me + k) % n_e},
        )

    for k in range(1, n_e):
        dcopy(k).start()
    score_back[1, pl.ds(me, 1)] = score_back[0, pl.ds(me, 1)]

    for k in range(1, n_z):
        larrival(k).wait_recv()
    low = low_all[0]
    for k in range(1, n_z):
        low = low + low_all[k]
    low = pick_row[0:1, :] * low
    for h in range(halves):
        b_out[:, h * width:(h + 1) * width] = adapter_scale * split_dot(low, own_rows[h])

    for k in range(1, n_e):
        darrival(k).wait_recv()
    firsts = jnp.zeros((1, tokens), jnp.float32)
    seconds = jnp.zeros((1, tokens), jnp.float32)
    for o in range(n_e):
        first, second = masks(meta[...], o * CAP)
        col = turned(score_back[1, o][0:1, :], CAP)[:, 0:1]
        firsts = firsts + jnp.sum(jnp.where(first, col, 0.0), axis=0, keepdims=True)
        seconds = seconds + jnp.sum(jnp.where(second, col, 0.0), axis=0, keepdims=True)
    w_out[0:1, :] = firsts
    w_out[1:2, :] = seconds

    def drain(chunk, carry):
        zs = chunk // halves

        @pl.when((zs <= z) & (z < n_z - 1))
        def _():
            zcopy(chunk, z + 1, zright).wait_send()

        @pl.when((zs >= z) & (z > 0))
        def _():
            zcopy(chunk, z - 1, zleft).wait_send()

        @pl.when(direct(chunk))
        def _():
            for k in range(1, n_x):
                xcopy(chunk, k).wait_send()

        for k in range(n_x):
            scopy(chunk, (x + k) % n_x).wait_send()
        return carry

    lax.fori_loop(0, items, drain, 0)
    if detour:
        pcopy().wait_send()
    for k in range(1, n_e):
        mcopy(k).wait_send()
        dcopy(k).wait_send()
    for k in range(1, n_z):
        lcopy(k).wait_send()
        ccopy(k).wait_send()

    def flush(n, carry):
        for copy in outs(n):
            copy.wait()
        return carry

    lax.fori_loop(0, tiles, flush, 0)


def body(
    output_gradient,
    routes,
    mixture_coefficients,
    gate_preactivation,
    up_projection_saved,
    down_matrix,
    lowrank_left_matrix,
    lowrank_right_matrix,
):
    n_e = lax.axis_size("expert")
    n_z = lax.axis_size("mp")
    tokens, span = output_gradient.shape
    halves = 2 if span % 256 == 0 else 1
    width = span // halves
    items = n_z * halves
    n_x = n_e // 2
    slots, units = gate_preactivation.shape[1:]
    rank = lowrank_left_matrix.shape[1]
    model = down_matrix.shape[2]
    tiles = units // TILE

    bf, f32 = jnp.bfloat16, jnp.float32
    anywhere = pl.BlockSpec(memory_space=pl.ANY)
    vmem = pl.BlockSpec(memory_space=pltpu.VMEM)
    dma = pltpu.SemaphoreType.DMA
    gate_grad, up_grad, a_grad, b_grad, scores = pl.pallas_call(
        functools.partial(kernel, n_z, n_e, halves),
        out_shape=(
            jax.ShapeDtypeStruct((slots, units), bf),
            jax.ShapeDtypeStruct((slots, units), bf),
            jax.ShapeDtypeStruct((rank, units), f32),
            jax.ShapeDtypeStruct((rank, span), f32),
            jax.ShapeDtypeStruct((2, tokens), f32),
        ),
        in_specs=[anywhere, vmem, vmem, anywhere, anywhere, anywhere, vmem, vmem],
        out_specs=(anywhere, anywhere, vmem, vmem, vmem),
        scratch_shapes=[
            pltpu.VMEM((items, n_e, tokens, width), bf),
            pltpu.VMEM((WBUFS, units, width), bf),
            pltpu.VMEM((slots, units), f32),
            pltpu.VMEM((slots, units), bf),
            pltpu.VMEM((slots, units), f32),
            pltpu.VMEM((slots, units), f32),
            pltpu.VMEM((slots, units), bf),
            pltpu.VMEM((slots, units), bf),
            pltpu.VMEM((slots, width), bf),
            pltpu.VMEM((halves, slots, width), bf),
            pltpu.VMEM((n_e, CAP, tokens), bf),
            pltpu.VMEM((8, tokens), f32),
            pltpu.VMEM((n_e, 8, tokens), f32),
            pltpu.VMEM((slots, 128), f32),
            pltpu.VMEM((8, slots), f32),
            pltpu.VMEM((rank, slots), f32),
            pltpu.VMEM((rank, slots), f32),
            pltpu.VMEM((n_z, rank, slots), f32),
            pltpu.VMEM((n_z, 8, slots), f32),
            pltpu.VMEM((2, n_e, 8, CAP), f32),
            pltpu.VMEM((slots, 128), f32),
            dma((halves,)),
            dma((WBUFS,)),
            dma((2,)),
            dma((2, tiles)),
            dma((items,)),
            dma((items,)),
            dma((items,)),
            dma((n_x - 1, items)),
            dma((n_x - 1, items)),
            dma((n_x, items)),
            dma((n_x, items)),
            dma((1,)),
            dma((1,)),
            dma((n_e - 1,)),
            dma((n_e - 1,)),
            dma((n_z - 1,)),
            dma((n_z - 1,)),
            dma((n_z - 1,)),
            dma((n_z - 1,)),
            dma((n_e - 1,)),
            dma((n_e - 1,)),
        ],
        compiler_params=pltpu.CompilerParams(
            collective_id=0, has_side_effects=True, vmem_limit_bytes=60 * 1024 * 1024
        ),
        cost_estimate=pl.CostEstimate(
            flops=2 * slots * units * model,
            bytes_accessed=2 * units * model,
            transcendentals=slots * units,
        ),
    )(
        output_gradient, routes.T, mixture_coefficients.T, gate_preactivation[0], up_projection_saved[0],
        down_matrix[0], lowrank_left_matrix[0], lowrank_right_matrix[0],
    )
    return gate_grad[None], up_grad[None], a_grad[None], b_grad[None], scores.T


def solution(mesh):
    placed = (
        P(("groups", "expert"), "mp"),
        P(("groups", "expert"), None),
        P(("groups", "expert"), None),
        P("expert", "groups", "mp"),
        P("expert", "groups", "mp"),
        P("expert", "mp", None),
        P("expert", None, "mp"),
        P("expert", None, None),
    )
    return jax.shard_map(
        body,
        mesh=mesh,
        in_specs=placed,
        out_specs=(
            P("expert", "groups", "mp"),
            P("expert", "groups", "mp"),
            P(("groups", "expert"), None, "mp"),
            P(("groups", "expert"), None, "mp"),
            P(("groups", "expert"), None),
        ),
        check_vma=False,
    )
```

```python
import functools

import jax
import jax.numpy as jnp
from jax import lax
from jax.experimental import pallas as pl
from jax.experimental.pallas import tpu as pltpu
from jax.sharding import PartitionSpec as P

CAP = 128
TILE = 256
LAG = 2
WBUFS = 4
MESH = pl.DeviceIdType.MESH

adapter_scale = 2.0


def contract_last(left, right):
    return lax.dot_general(
        left, right, (((1,), (1,)), ((), ())), preferred_element_type=jnp.float32
    )


def split_dot(left, right):
    high = left.astype(jnp.bfloat16)
    low = (left - high.astype(jnp.float32)).astype(jnp.bfloat16)
    return jnp.dot(high, right, preferred_element_type=jnp.float32) + jnp.dot(
        low, right, preferred_element_type=jnp.float32
    )


def turned(row, count):
    return jnp.transpose(jnp.broadcast_to(row, (count, row.shape[1])))


def kernel(
    n_z, n_e, halves,
    tok, routes, mix, gate, up, weight, left_m, right_m,
    gate_out, up_out, a_out, b_out, w_out,
    tbuf, wbuf, dh, hid, coef, act, gbuf, ubuf, rows, own_rows, dmat, meta, metas,
    pick_col, pick_row, back_t, low_acc, low_all, score_all, score_back, score_acc,
    load_sem, w_sem, io_sem, out_sem, zrecv, zright, zleft, xsend, xrecv, ssend, srecv,
    psend, precv, msend, mrecv, lsend, lrecv, csend, crecv, dsend, drecv,
):
    me = lax.axis_index("expert")
    z = lax.axis_index("mp")
    n_x = n_e // 2
    x, core = me // 2, me % 2
    width = tok.shape[1] // halves
    items = n_z * halves
    hidden_units = gate.shape[1]
    tiles = hidden_units // TILE
    wide_tile = min(hidden_units, 1024)
    detour = False
    pair = z + 1 - 2 * (z % 2)
    late_at = jnp.where((z % 2 == 1) | (z == 0), 3, 5)

    def remote(src, dst, send, recv, where):
        return pltpu.make_async_remote_copy(
            src_ref=src, dst_ref=dst, send_sem=send, recv_sem=recv,
            device_id=where, device_id_type=MESH,
        )

    def zcopy(chunk, to, send):
        block = tbuf.at[chunk, me]
        return remote(block, block, send.at[chunk], zrecv.at[chunk], {"mp": to})

    def xcopy(chunk, k):
        block = tbuf.at[chunk, me]
        to = ((x + k) % n_x) * 2 + core
        return remote(block, block, xsend.at[k - 1, chunk], xrecv.at[k - 1, chunk], {"expert": to})

    def xarrival(chunk, k):
        block = tbuf.at[chunk, ((x + n_x - k) % n_x) * 2 + core]
        to = ((x + k) % n_x) * 2 + core
        return remote(block, block, xsend.at[k - 1, chunk], xrecv.at[k - 1, chunk], {"expert": to})

    def scopy(chunk, xs):
        block = tbuf.at[chunk, xs * 2 + core]
        return remote(block, block, ssend.at[xs, chunk], srecv.at[xs, chunk], {"expert": x * 2 + 1 - core})

    def sarrival(chunk, xs):
        block = tbuf.at[chunk, xs * 2 + 1 - core]
        return remote(block, block, ssend.at[xs, chunk], srecv.at[xs, chunk], {"expert": x * 2 + 1 - core})

    def direct(chunk):
        return (chunk != pair * halves + 1) if detour else (chunk >= 0)

    def pcopy():
        block = tbuf.at[z * halves + 1, (1 - x) * 2 + core]
        return remote(block, block, psend.at[0], precv.at[0], {"mp": pair})

    def parrival():
        block = tbuf.at[pair * halves + 1, (1 - x) * 2 + core]
        return remote(block, block, psend.at[0], precv.at[0], {"mp": pair})

    def spread(chunk):
        @pl.when(direct(chunk))
        def _():
            for k in range(1, n_x):
                xcopy(chunk, k).start()

        scopy(chunk, x).start()

    def item_chunk(i):
        if detour:
            i = jnp.where(i < late_at, i, jnp.where(i == items - 1, late_at, i + 1))
        j, h = i // halves, i % halves
        m = jnp.minimum(z, n_z - 1 - z)
        near = jnp.where(j % 2 == 1, z - (j + 1) // 2, z + j // 2)
        far = jnp.where(z > n_z - 1 - z, z - (j - m), z + (j - m))
        return jnp.where(j <= 2 * m, near, far) * halves + h

    def load(h):
        return pltpu.make_async_copy(
            tok.at[:, pl.ds(h * width, width)], tbuf.at[z * halves + h, me], load_sem.at[h]
        )

    def wload(i):
        chunk = item_chunk(i)
        return pltpu.make_async_copy(
            weight.at[:, pl.ds(pl.multiple_of(chunk * width, 128), width)],
            wbuf.at[i % WBUFS],
            w_sem.at[i % WBUFS],
        )

    for h in range(halves):
        load(h).start()
    gate_in = pltpu.make_async_copy(gate, gbuf, io_sem.at[0])
    up_in = pltpu.make_async_copy(up, ubuf, io_sem.at[1])
    gate_in.start()
    up_in.start()

    barrier = pltpu.get_barrier_semaphore()
    for k in range(1, n_e):
        pl.semaphore_signal(barrier, inc=1, device_id={"expert": (me + k) % n_e}, device_id_type=MESH)
    for k in range(1, n_z):
        pl.semaphore_signal(barrier, inc=1, device_id={"mp": (z + k) % n_z}, device_id_type=MESH)
    pl.semaphore_wait(barrier, n_e + n_z - 2)

    def mcopy(k):
        return remote(meta, metas.at[me], msend.at[k - 1], mrecv.at[k - 1], {"expert": (me + k) % n_e})

    def marrival(k):
        return remote(
            meta, metas.at[(me + n_e - k) % n_e], msend.at[k - 1], mrecv.at[k - 1],
            {"expert": (me + k) % n_e},
        )

    for h in range(halves):
        chunk = z * halves + h
        load(h).wait()

        @pl.when(z < n_z - 1)
        def _():
            zcopy(chunk, z + 1, zright).start()

        @pl.when(z > 0)
        def _():
            zcopy(chunk, z - 1, zleft).start()

        spread(chunk)
    for i in range(WBUFS):
        wload(i).start()
    tokens = routes.shape[1]
    named = routes[...].astype(jnp.float32)
    wanted = lax.broadcasted_iota(jnp.int32, (16, tokens), 0).astype(jnp.float32)
    hot = jnp.where(wanted == named[0:1, :], 1.0, 0.0) + jnp.where(wanted == named[1:2, :], 1.0, 0.0)
    earlier = (
        lax.broadcasted_iota(jnp.int32, (tokens, tokens), 0)
        < lax.broadcasted_iota(jnp.int32, (tokens, tokens), 1)
    )
    before = jnp.dot(
        hot.astype(jnp.bfloat16),
        jnp.where(earlier, 1.0, 0.0).astype(jnp.bfloat16),
        preferred_element_type=jnp.float32,
    )
    meta[...] = jnp.zeros_like(meta)
    for k in range(2):
        one = named[k:k + 1, :]
        place = jnp.sum(jnp.where(wanted == one, before, 0.0), axis=0, keepdims=True)
        meta[k:k + 1, :] = one * CAP + place
    meta[2:4, :] = mix[...].astype(jnp.float32)
    for k in range(1, n_e):
        mcopy(k).start()
    metas[pl.ds(me, 1)] = meta[...][None]
    low_acc[...] = jnp.zeros_like(low_acc)
    back_t[...] = jnp.zeros_like(back_t)
    for k in range(1, n_e):
        marrival(k).wait_recv()
    slot = lax.broadcasted_iota(jnp.int32, (CAP, tokens), 0)

    def masks(keys, base):
        numbers = (slot + base).astype(jnp.float32)
        return numbers == keys[0:1, :], numbers == keys[1:2, :]

    for o in range(n_e):
        keys = metas[o]
        first, second = masks(keys, me * CAP)
        dmat[o] = (jnp.where(first, 1.0, 0.0) + jnp.where(second, 1.0, 0.0)).astype(jnp.bfloat16)
        col = jnp.sum(
            jnp.where(first, keys[2:3, :], 0.0) + jnp.where(second, keys[3:4, :], 0.0),
            axis=1, keepdims=True,
        )
        wide = jnp.broadcast_to(col, (CAP, 128))
        pick_col[o * CAP:(o + 1) * CAP, :] = wide
        pick_row[:, o * CAP:(o + 1) * CAP] = jnp.transpose(wide)[0:8, :]
    gate_in.wait()
    up_in.wait()

    def lcopy(k):
        return remote(low_acc, low_all.at[z], lsend.at[k - 1], lrecv.at[k - 1], {"mp": (z + k) % n_z})

    def larrival(k):
        return remote(
            low_acc, low_all.at[(z + n_z - k) % n_z], lsend.at[k - 1], lrecv.at[k - 1],
            {"mp": (z + k) % n_z},
        )

    def prepare(n):
        cols = pl.ds(pl.multiple_of(n * TILE, TILE), TILE)
        g = gbuf[:, cols].astype(jnp.float32)
        u = ubuf[:, cols].astype(jnp.float32)
        sigma = jax.nn.sigmoid(g)
        a = g * sigma
        hidden = (a * u).astype(jnp.bfloat16)
        hid[:, cols] = hidden
        act[:, cols] = a
        coef[:, cols] = u * sigma * (1.0 + g * (1.0 - sigma))
        dh[:, cols] = jnp.zeros((dh.shape[0], TILE), jnp.float32)
        low_acc[...] += contract_last(left_m[:, cols], hidden)

    per_step = -(-tiles // LAG)

    def product(i):
        chunk = item_chunk(i)
        @pl.when(direct(chunk))
        def _():
            for k in range(1, n_x):
                xarrival(chunk, k).wait_recv()

        if detour:
            @pl.when(chunk == pair * halves + 1)
            def _():
                parrival().wait_recv()

        for k in range(1, n_x):
            scopy(chunk, (x + n_x - k) % n_x).start()
        for k in range(n_x):
            sarrival(chunk, (x + n_x - k) % n_x).wait_recv()
        for o in range(n_e):
            rows[o * CAP:(o + 1) * CAP, :] = jnp.dot(
                dmat[o], tbuf[chunk, o], preferred_element_type=jnp.float32
            ).astype(jnp.bfloat16)

        @pl.when(i < halves)
        def _():
            own_rows[i % halves] = rows[...]

        back_t[...] += contract_last(
            rows[...], right_m[:, pl.ds(pl.multiple_of(chunk * width, 128), width)]
        )
        wload(i).wait()

        def tile(n, carry):
            at = pl.ds(pl.multiple_of(n * wide_tile, TILE), wide_tile)
            dh[:, at] += contract_last(rows[...], wbuf[i % WBUFS, at, :])
            return carry

        lax.fori_loop(0, hidden_units // wide_tile, tile, 0)

        @pl.when(i + WBUFS < items)
        def _():
            wload(i + WBUFS).start()

    def right_sums():
        for k in range(1, n_z):
            larrival(k).wait_recv()
        low = low_all[0]
        for k in range(1, n_z):
            low = low + low_all[k]
        low = pick_row[0:1, :] * low
        for h in range(halves):
            b_out[:, h * width:(h + 1) * width] = adapter_scale * split_dot(low, own_rows[h])

    def step(t, carry):
        @pl.when((t >= halves) & (t < items))
        def _():
            d, h = t // halves, t % halves

            @pl.when(z - d >= 0)
            def _():
                chunk = (z - d) * halves + h
                zcopy(chunk, z, zright).wait_recv()

                @pl.when(z < n_z - 1)
                def _():
                    zcopy(chunk, z + 1, zright).start()

                spread(chunk)

            @pl.when(z + d < n_z)
            def _():
                chunk = (z + d) * halves + h
                zcopy(chunk, z, zleft).wait_recv()

                @pl.when(z > 0)
                def _():
                    zcopy(chunk, z - 1, zleft).start()

                spread(chunk)

        if detour:
            @pl.when(t == items - halves - 1)
            def _():
                pcopy().start()

        @pl.when(t < LAG)
        def _():
            def some(n, carry):
                prepare(n)
                return carry

            lax.fori_loop(t * per_step, jnp.minimum((t + 1) * per_step, tiles), some, 0)

        @pl.when(t >= LAG)
        def _():
            product(t - LAG)

        @pl.when(t == items - 1)
        def _():
            right_sums()

        return carry

    lax.fori_loop(0, LAG, step, 0)
    low_all[pl.ds(z, 1)] = low_acc[...][None]
    for k in range(1, n_z):
        lcopy(k).start()
    lax.fori_loop(LAG, items + LAG, step, 0)

    rounded = back_t[...].astype(jnp.bfloat16).astype(jnp.float32)
    back = jnp.transpose(rounded)
    back_col = (adapter_scale * rounded).astype(jnp.bfloat16)
    pick = jnp.concatenate([pick_col[...]] * (TILE // 128), axis=1)
    score_acc[...] = jnp.zeros_like(score_acc)

    def outs(n):
        cols = pl.ds(pl.multiple_of(n * TILE, TILE), TILE)
        return (
            pltpu.make_async_copy(gbuf.at[:, cols], gate_out.at[:, cols], out_sem.at[0, n]),
            pltpu.make_async_copy(ubuf.at[:, cols], up_out.at[:, cols], out_sem.at[1, n]),
        )

    def finish(n, carry):
        cols = pl.ds(pl.multiple_of(n * TILE, TILE), TILE)
        d = dh[:, cols] + jnp.dot(
            back_col, left_m[:, cols], preferred_element_type=jnp.float32
        )
        prod = hid[:, cols].astype(jnp.float32) * d
        total = prod[:, 0:128]
        for q in range(1, TILE // 128):
            total = total + prod[:, q * 128:(q + 1) * 128]
        score_acc[...] += total
        scaled = pick * d
        gbuf[:, cols] = (scaled * coef[:, cols]).astype(jnp.bfloat16)
        ubuf[:, cols] = (scaled * act[:, cols]).astype(jnp.bfloat16)
        for copy in outs(n):
            copy.start()
        return carry

    lax.fori_loop(0, tiles, finish, 0)

    mine = jnp.sum(jnp.transpose(score_acc[...]), axis=0, keepdims=True)
    score_all[pl.ds(z, 1)] = jnp.broadcast_to(mine, (8, mine.shape[1]))[None]

    def ccopy(k):
        block = score_all.at[z]
        return remote(block, block, csend.at[k - 1], crecv.at[k - 1], {"mp": (z + k) % n_z})

    def carrival(k):
        block = score_all.at[(z + n_z - k) % n_z]
        return remote(block, block, csend.at[k - 1], crecv.at[k - 1], {"mp": (z + k) % n_z})

    for k in range(1, n_z):
        ccopy(k).start()

    a_out[...] = adapter_scale * split_dot(pick_row[0:1, :] * back, hid[...])

    for k in range(1, n_z):
        carrival(k).wait_recv()
    whole = score_all[0]
    for k in range(1, n_z):
        whole = whole + score_all[k]
    for o in range(n_e):
        score_back[0, o] = whole[:, o * CAP:(o + 1) * CAP]

    def dcopy(k):
        to = (me + k) % n_e
        return remote(
            score_back.at[0, to], score_back.at[1, me], dsend.at[k - 1], drecv.at[k - 1], {"expert": to}
        )

    def darrival(k):
        return remote(
            score_back.at[0, (me + k) % n_e], score_back.at[1, (me + n_e - k) % n_e],
            dsend.at[k - 1], drecv.at[k - 1], {"expert": (me + k) % n_e},
        )

    for k in range(1, n_e):
        dcopy(k).start()
    score_back[1, pl.ds(me, 1)] = score_back[0, pl.ds(me, 1)]

    for k in range(1, n_e):
        darrival(k).wait_recv()
    firsts = jnp.zeros((1, tokens), jnp.float32)
    seconds = jnp.zeros((1, tokens), jnp.float32)
    for o in range(n_e):
        first, second = masks(meta[...], o * CAP)
        col = turned(score_back[1, o][0:1, :], CAP)[:, 0:1]
        firsts = firsts + jnp.sum(jnp.where(first, col, 0.0), axis=0, keepdims=True)
        seconds = seconds + jnp.sum(jnp.where(second, col, 0.0), axis=0, keepdims=True)
    w_out[0:1, :] = firsts
    w_out[1:2, :] = seconds

    def drain(chunk, carry):
        zs = chunk // halves

        @pl.when((zs <= z) & (z < n_z - 1))
        def _():
            zcopy(chunk, z + 1, zright).wait_send()

        @pl.when((zs >= z) & (z > 0))
        def _():
            zcopy(chunk, z - 1, zleft).wait_send()

        @pl.when(direct(chunk))
        def _():
            for k in range(1, n_x):
                xcopy(chunk, k).wait_send()

        for k in range(n_x):
            scopy(chunk, (x + k) % n_x).wait_send()
        return carry

    lax.fori_loop(0, items, drain, 0)
    if detour:
        pcopy().wait_send()
    for k in range(1, n_e):
        mcopy(k).wait_send()
        dcopy(k).wait_send()
    for k in range(1, n_z):
        lcopy(k).wait_send()
        ccopy(k).wait_send()

    def flush(n, carry):
        for copy in outs(n):
            copy.wait()
        return carry

    lax.fori_loop(0, tiles, flush, 0)


def body(
    output_gradient,
    routes,
    mixture_coefficients,
    gate_preactivation,
    up_projection_saved,
    down_matrix,
    lowrank_left_matrix,
    lowrank_right_matrix,
):
    n_e = lax.axis_size("expert")
    n_z = lax.axis_size("mp")
    tokens, span = output_gradient.shape
    halves = 2 if span % 256 == 0 else 1
    width = span // halves
    items = n_z * halves
    n_x = n_e // 2
    slots, units = gate_preactivation.shape[1:]
    rank = lowrank_left_matrix.shape[1]
    model = down_matrix.shape[2]
    tiles = units // TILE

    bf, f32 = jnp.bfloat16, jnp.float32
    anywhere = pl.BlockSpec(memory_space=pl.ANY)
    vmem = pl.BlockSpec(memory_space=pltpu.VMEM)
    dma = pltpu.SemaphoreType.DMA
    gate_grad, up_grad, a_grad, b_grad, scores = pl.pallas_call(
        functools.partial(kernel, n_z, n_e, halves),
        out_shape=(
            jax.ShapeDtypeStruct((slots, units), bf),
            jax.ShapeDtypeStruct((slots, units), bf),
            jax.ShapeDtypeStruct((rank, units), f32),
            jax.ShapeDtypeStruct((rank, span), f32),
            jax.ShapeDtypeStruct((2, tokens), f32),
        ),
        in_specs=[anywhere, vmem, vmem, anywhere, anywhere, anywhere, vmem, vmem],
        out_specs=(anywhere, anywhere, vmem, vmem, vmem),
        scratch_shapes=[
            pltpu.VMEM((items, n_e, tokens, width), bf),
            pltpu.VMEM((WBUFS, units, width), bf),
            pltpu.VMEM((slots, units), f32),
            pltpu.VMEM((slots, units), bf),
            pltpu.VMEM((slots, units), f32),
            pltpu.VMEM((slots, units), f32),
            pltpu.VMEM((slots, units), bf),
            pltpu.VMEM((slots, units), bf),
            pltpu.VMEM((slots, width), bf),
            pltpu.VMEM((halves, slots, width), bf),
            pltpu.VMEM((n_e, CAP, tokens), bf),
            pltpu.VMEM((8, tokens), f32),
            pltpu.VMEM((n_e, 8, tokens), f32),
            pltpu.VMEM((slots, 128), f32),
            pltpu.VMEM((8, slots), f32),
            pltpu.VMEM((slots, rank), f32),
            pltpu.VMEM((rank, slots), f32),
            pltpu.VMEM((n_z, rank, slots), f32),
            pltpu.VMEM((n_z, 8, slots), f32),
            pltpu.VMEM((2, n_e, 8, CAP), f32),
            pltpu.VMEM((slots, 128), f32),
            dma((halves,)),
            dma((WBUFS,)),
            dma((2,)),
            dma((2, tiles)),
            dma((items,)),
            dma((items,)),
            dma((items,)),
            dma((n_x - 1, items)),
            dma((n_x - 1, items)),
            dma((n_x, items)),
            dma((n_x, items)),
            dma((1,)),
            dma((1,)),
            dma((n_e - 1,)),
            dma((n_e - 1,)),
            dma((n_z - 1,)),
            dma((n_z - 1,)),
            dma((n_z - 1,)),
            dma((n_z - 1,)),
            dma((n_e - 1,)),
            dma((n_e - 1,)),
        ],
        compiler_params=pltpu.CompilerParams(
            collective_id=0, has_side_effects=True, vmem_limit_bytes=60 * 1024 * 1024
        ),
        cost_estimate=pl.CostEstimate(
            flops=2 * slots * units * model,
            bytes_accessed=2 * units * model,
            transcendentals=slots * units,
        ),
    )(
        output_gradient, routes.T, mixture_coefficients.T, gate_preactivation[0], up_projection_saved[0],
        down_matrix[0], lowrank_left_matrix[0], lowrank_right_matrix[0],
    )
    return gate_grad[None], up_grad[None], a_grad[None], b_grad[None], scores.T


def solution(mesh):
    placed = (
        P(("groups", "expert"), "mp"),
        P(("groups", "expert"), None),
        P(("groups", "expert"), None),
        P("expert", "groups", "mp"),
        P("expert", "groups", "mp"),
        P("expert", "mp", None),
        P("expert", None, "mp"),
        P("expert", None, None),
    )
    return jax.shard_map(
        body,
        mesh=mesh,
        in_specs=placed,
        out_specs=(
            P("expert", "groups", "mp"),
            P("expert", "groups", "mp"),
            P(("groups", "expert"), None, "mp"),
            P(("groups", "expert"), None, "mp"),
            P(("groups", "expert"), None),
        ),
        check_vma=False,
    )
```
